512 devices in a mesh: blk: 128 (over y, x_lo, z), grp: 4 (over x_hi, core).
Axes of the slice: x: 4 (x_hi: 2, x_lo: 2; x = x_hi * 2 + x_lo), y: 8, z: 8, core: 2. Of those that a mesh axis runs over, the one named last changes fastest.
Arguments:
- camera_vectors: bfloat16 [98304, 768], P(('blk', 'grp')), may hold values from -2 to 2
- command_vectors: bfloat16 [98304, 768], P(('blk', 'grp')), may hold values from -2 to 2
- sharpness_array: float32 [1], replicated, may hold values from 4 to 12
- offset_shift_array: float32 [1], replicated, may hold values from -3 to -1
Outputs:
- grad_frames: float32 [98304, 768], P(('blk', 'grp'))
- grad_instructions: float32 [98304, 768], P(('blk', 'grp'))
The draws below stay inside these ranges and needn't reach their ends.
All inputs are finite; a program needn't handle non-finite values.
Results may differ from the reference program's by a relative error of at most 0.014.
Values may be sent and summed in bfloat16 or wider, within the bound.
A program may use at most 64 MiB of HBM per device.

```python
import math
import jax
import jax.numpy as jnp
from jax import lax

D = 768
R = 192
STEPS = 6
TOTAL = 98304
N_BLK = 128
N_GRP = 4


def paired_base(key):
    return jax.random.normal(key, (TOTAL, D), jnp.float32)


def rough_rows(key, base, weight):
    first, second_term, third = jax.random.split(key, 3)
    noise = jax.random.normal(first, (TOTAL, D), jnp.float32)
    per_entry_factor = jnp.exp(jax.random.uniform(second_term, (TOTAL, 1), jnp.float32, 0.0, math.log(10.0)))
    col_scale = jnp.exp(jax.random.uniform(third, (1, D), jnp.float32, 0.0, math.log(10.0)))
    values = (weight * base + noise) * per_entry_factor * col_scale * 0.1 / math.sqrt(D)
    return jnp.clip(values, -2.0, 2.0)


def draw_camera_vectors(key, part):
    base = paired_base(key)
    key = jax.random.fold_in(key, 11)
    return rough_rows(key, base, 1.0).astype(jnp.bfloat16)


def draw_command_vectors(key, part):
    base = paired_base(key)
    key = jax.random.fold_in(key, 23)
    return rough_rows(key, base, 0.8).astype(jnp.bfloat16)


def setup_inputs(seed: int = 0) -> dict:
    keys = jax.random.split(jax.random.key(seed), 5)
    return {
        "camera_vectors": draw_camera_vectors(jax.random.fold_in(keys[4], 71), 0),
        "command_vectors": draw_command_vectors(jax.random.fold_in(keys[4], 71), 0),
        "sharpness_array": jnp.clip(jax.random.uniform(keys[2], (1,), jnp.float32, 4.0, 12.0), 4.0, 12.0),
        "offset_shift_array": jnp.clip(jax.random.uniform(keys[3], (1,), jnp.float32, -3.0, -1.0), -3.0, -1.0),
    }


def unit_rows(values):
    wide = values.astype(jnp.float32)
    scale = lax.rsqrt(lax.optimization_barrier(jnp.sum(wide * wide, axis=-1, keepdims=True)) + 1e-06)
    return (wide * scale, scale)

def back_rows(unit, scale, grad):
    return scale * (grad - unit * lax.optimization_barrier(jnp.sum(unit * grad, axis=-1, keepdims=True)))

def reference(camera_vectors, command_vectors, sharpness_array, offset_shift_array):
    unit_x, inv_x = unit_rows(camera_vectors)
    unit_y, inv_y = unit_rows(command_vectors)
    block = R * N_GRP
    xb = unit_x.astype(jnp.bfloat16).reshape(N_BLK, block, D)
    yb = unit_y.astype(jnp.bfloat16).reshape(N_BLK, block, D)
    score_multiplier = sharpness_array[0]
    logit_bias = offset_shift_array[0]
    lowest = -(STEPS // 2)
    diagonal = jnp.eye(block, dtype=jnp.float32)

    def visit(carry, index):
        xblock = xb[index]
        grad_x = jnp.zeros((block, D), jnp.float32)
        for offset in range(lowest, lowest + STEPS):
            target_labels = jnp.mod(index + offset, N_BLK).astype(jnp.int32)
            yblock = yb[target_labels]
            logits = score_multiplier * lax.dot_general(xblock, yblock, (((1,), (1,)), ((), ())), preferred_element_type=jnp.float32) + logit_bias
            if offset == 0:
                label = 2.0 * diagonal - 1.0
            else:
                label = -jnp.ones_like(logits)
            coef = (-label * score_multiplier * jax.nn.sigmoid(-label * logits)).astype(jnp.bfloat16)
            grad_x = grad_x + jnp.dot(coef, yblock, preferred_element_type=jnp.float32)
            block_pieces = jnp.einsum('grk,grd->gkd', coef.reshape(N_GRP, R, block).astype(jnp.float32), xblock.reshape(N_GRP, R, D).astype(jnp.float32))
            block_pieces = block_pieces.astype(jnp.bfloat16).astype(jnp.float32)
            carry = carry.at[target_labels].add(lax.optimization_barrier(jnp.sum(block_pieces, axis=0)))
        return (carry, grad_x)
    start = jnp.zeros((N_BLK, block, D), jnp.float32)
    total_y, parts_x = lax.scan(visit, start, jnp.arange(N_BLK, dtype=jnp.int32))
    grad_frames = back_rows(unit_x, inv_x, parts_x.reshape(TOTAL, D))
    grad_instructions = back_rows(unit_y, inv_y, total_y.reshape(TOTAL, D))
    return (grad_frames, grad_instructions)
```

```python
import functools

import jax
import jax.numpy as jnp
from jax import lax
from jax.experimental import pallas as pl
from jax.experimental.pallas import tpu as pltpu
from jax.sharding import PartitionSpec as P

MESH = pl.DeviceIdType.MESH
R = 192
D = 768
RUN = 8
N = 4
C = R // N
F32 = jnp.float32
BF16 = jnp.bfloat16

OWN, M1, M2, M3, P1, P2 = 0, 1, 2, 3, 4, 5


def inv_norm(wide):
    return lax.rsqrt(jnp.sum(wide * wide, axis=-1, keepdims=True) + 1e-06)


def back_rows(values, grad):
    wide = values.astype(F32)
    scale = inv_norm(wide)
    unit = wide * scale
    return scale * (grad - unit * jnp.sum(unit * grad, axis=-1, keepdims=True))


def kernel(
    nb, x_ref, y_ref, s_ref, b_ref, gx_ref, gy_ref,
    xf, ys, ct, part, accs, accr, gsend, grecv, xsend, xrecv, gown,
    ysend, yrecv, asend, arecv, gs, gr,
):
    b = lax.axis_index("blk")
    g = lax.axis_index("grp")
    core = lax.rem(g, 2)
    spot = lax.rem(b, 2 * RUN)
    last = jnp.where(core == 0, 2 * RUN - 1, RUN - 1)
    first = jnp.where(core == 0, 0, RUN)
    partner = lax.rem(g + 2, 4)
    nxt = (lax.rem(b + 1, nb), jnp.where(spot == last, partner, g))
    prv = (lax.rem(b + nb - 1, nb), jnp.where(spot == first, partner, g))
    xp = (b, partner)
    cp = (b, g + 1 - 2 * core)

    barrier = pltpu.get_barrier_semaphore()
    for who in (nxt, prv, xp, cp):
        pl.semaphore_signal(barrier, inc=1, device_id=who, device_id_type=MESH)

    def rows(slot, c):
        return pl.ds(pl.multiple_of(slot * R + c * C, 16), C)

    def copy(src, dst, ssem, rsem, who):
        return pltpu.make_async_remote_copy(
            src_ref=src, dst_ref=dst, send_sem=ssem, recv_sem=rsem, device_id=who, device_id_type=MESH
        )

    kinds = ((OWN, M1, nxt), (M1, M2, nxt), (M2, M3, nxt), (OWN, P1, prv), (P1, P2, prv))

    def piece(kind, c):
        src, dst, who = kinds[kind]
        return copy(ys.at[rows(src, c)], ys.at[rows(dst, c)], ysend.at[kind, c], yrecv.at[kind, c], who)

    def acc(kind, c):
        who = prv if kind < 3 else nxt
        return copy(accs.at[rows(kind, c)], accr.at[rows(kind, c)], asend.at[kind, c], arecv.at[kind, c], who)

    def block(k, count=1):
        return pl.ds(k * R, count * R)

    gather_x = copy(xf.at[block(0)], xf.at[block(1)], gs.at[0], gr.at[0], xp)
    gather_c = copy(xf.at[block(0)], xf.at[block(2)], gs.at[1], gr.at[1], cp)
    gather_d = copy(xf.at[block(1)], xf.at[block(3)], gs.at[2], gr.at[2], cp)
    reduce_c = copy(gsend, grecv, gs.at[3], gr.at[3], cp)
    reduce_x = copy(xsend, xrecv, gs.at[4], gr.at[4], xp)

    def loop(body):
        lax.fori_loop(0, N, lambda c, _: (body(c), 0)[1], 0)

    wide = y_ref[...].astype(F32)
    ys[block(OWN)] = (wide * inv_norm(wide)).astype(BF16)
    pl.semaphore_wait(barrier, 4)

    @loop
    def _(c):
        piece(0, c).start()
        piece(3, c).start()

    wide = x_ref[...].astype(F32)
    xf[block(0)] = (wide * inv_norm(wide)).astype(BF16)
    gather_x.start()
    gather_c.start()

    @loop
    def _(c):
        piece(0, c).wait_recv()
        piece(1, c).start()
        piece(3, c).wait_recv()
        piece(4, c).start()

    gather_x.wait_recv()
    gather_d.start()
    gather_c.wait_recv()
    gather_d.wait_recv()

    scale = s_ref[0]
    bias = b_ref[0]

    def task(slot, c):
        y = ys[rows(slot, c)]
        dots = lax.dot_general(y, xf[...], (((1,), (1,)), ((), ())), preferred_element_type=F32)
        z = scale * dots + bias
        if slot == OWN:
            here = lax.broadcasted_iota(jnp.int32, (C, 4 * R), 1) == (
                lax.broadcasted_iota(jnp.int32, (C, 4 * R), 0) + c * C
            )
            sign = jnp.where(here, -1.0, 1.0).astype(F32)
            coef = sign * scale / (1.0 + jnp.exp(-sign * z))
        else:
            coef = scale / (1.0 + jnp.exp(-z))
        coef = coef.astype(BF16)
        ct[rows(slot, c)] = coef
        return jnp.dot(coef, xf[...], preferred_element_type=F32)

    @loop
    def _(c):
        piece(1, c).wait_recv()
        piece(2, c).start()
        part[rows(0, c)] = task(OWN, c)
        part[rows(1, c)] = task(M1, c)
        piece(4, c).wait_recv()
        accs[rows(3, c)] = task(P2, c).astype(BF16)

    @loop
    def _(c):
        piece(2, c).wait_recv()
        accs[rows(0, c)] = task(M3, c).astype(BF16)
        acc(0, c).start()
        acc(3, c).start()
        part[rows(2, c)] = task(M2, c)
        part[rows(3, c)] = task(P1, c)

    def pass_on(src, mine, dst, c):
        acc(src, c).wait_recv()
        accs[rows(dst, c)] = (part[rows(mine, c)] + accr[rows(src, c)].astype(F32)).astype(BF16)
        acc(dst, c).start()

    @loop
    def _(c):
        pass_on(0, 2, 1, c)
        pass_on(3, 3, 4, c)

    def grads(lo):
        return lax.dot_general(
            ct[:, lo * R : (lo + 2) * R], ys[...], (((0,), (0,)), ((), ())), preferred_element_type=F32
        )

    gsend[...] = grads(2).astype(BF16)
    reduce_c.start()
    gown[...] = grads(0)
    reduce_c.wait_recv()
    xsend[...] = (gown[block(1)] + grecv[block(1)].astype(F32)).astype(BF16)
    reduce_x.start()

    @loop
    def _(c):
        pass_on(1, 1, 2, c)

    @loop
    def _(c):
        acc(4, c).wait_recv()
        acc(2, c).wait_recv()
        grad = part[rows(0, c)] + accr[rows(4, c)].astype(F32) + accr[rows(2, c)].astype(F32)
        gy_ref[rows(0, c)] = back_rows(y_ref[rows(0, c)], grad)

    reduce_x.wait_recv()
    total = gown[block(0)] + grecv[block(0)].astype(F32) + xrecv[...].astype(F32)
    gx_ref[...] = back_rows(x_ref[...], total)

    @loop
    def _(c):
        for kind in range(5):
            piece(kind, c).wait_send()
            acc(kind, c).wait_send()

    for one in (gather_x, gather_c, gather_d, reduce_c, reduce_x):
        one.wait_send()


def solution(mesh):
    nb = mesh.shape["blk"]

    def local(x, y, s, b):
        vmem = pl.BlockSpec(memory_space=pltpu.VMEM)
        smem = pl.BlockSpec(memory_space=pltpu.SMEM)
        dma = pltpu.SemaphoreType.DMA
        return pl.pallas_call(
            functools.partial(kernel, nb),
            out_shape=[jax.ShapeDtypeStruct((R, D), F32)] * 2,
            in_specs=[vmem, vmem, smem, smem],
            out_specs=[vmem, vmem],
            scratch_shapes=[
                pltpu.VMEM((4 * R, D), BF16),
                pltpu.VMEM((6 * R, D), BF16),
                pltpu.VMEM((6 * R, 4 * R), BF16),
                pltpu.VMEM((4 * R, D), F32),
                pltpu.VMEM((5 * R, D), BF16),
                pltpu.VMEM((5 * R, D), BF16),
                pltpu.VMEM((2 * R, D), BF16),
                pltpu.VMEM((2 * R, D), BF16),
                pltpu.VMEM((R, D), BF16),
                pltpu.VMEM((R, D), BF16),
                pltpu.VMEM((2 * R, D), F32),
                dma((5, N)),
                dma((5, N)),
                dma((5, N)),
                dma((5, N)),
                dma((5,)),
                dma((5,)),
            ],
            compiler_params=pltpu.CompilerParams(
                collective_id=0, has_side_effects=True, vmem_limit_bytes=48 * 2**20
            ),
            cost_estimate=pl.CostEstimate(flops=4 * 10**9, bytes_accessed=2 * 10**6, transcendentals=10**6),
        )(x, y, s, b)

    spec = P(("blk", "grp"), None)
    return jax.shard_map(
        local, mesh=mesh, in_specs=(spec, spec, P(), P()), out_specs=(spec, spec), check_vma=False
    )
```

```python
import functools

import jax
import jax.numpy as jnp
from jax import lax
from jax.experimental import pallas as pl
from jax.experimental.pallas import tpu as pltpu
from jax.sharding import PartitionSpec as P

MESH = pl.DeviceIdType.MESH
R = 192
D = 768
RUN = 8
N = 4
G = 1
C = R // N
F32 = jnp.float32
BF16 = jnp.bfloat16

OWN, M1, P1, P2, M2, M3 = 0, 1, 2, 3, 4, 5


def inv_norm(wide):
    return lax.rsqrt(jnp.sum(wide * wide, axis=-1, keepdims=True) + 1e-06)


def back_rows(values, grad):
    wide = values.astype(F32)
    scale = inv_norm(wide)
    unit = wide * scale
    return scale * (grad - unit * jnp.sum(unit * grad, axis=-1, keepdims=True))


def kernel(
    nb, x_hbm, y_hbm, s_ref, b_ref, gx_ref, gy_ref,
    x_ref, y_ref, xf, ys, ct, part, accs, accr, gsend, grecv, xsend, xrecv, gown,
    ysend, yrecv, asend, arecv, gs, gr, ls,
):
    b = lax.axis_index("blk")
    g = lax.axis_index("grp")
    core = lax.rem(g, 2)
    spot = lax.rem(b, 2 * RUN)
    last = jnp.where(core == 0, 2 * RUN - 1, RUN - 1)
    first = jnp.where(core == 0, 0, RUN)
    partner = lax.rem(g + 2, 4)
    nxt = (lax.rem(b + 1, nb), jnp.where(spot == last, partner, g))
    prv = (lax.rem(b + nb - 1, nb), jnp.where(spot == first, partner, g))
    xp = (b, partner)
    cp = (b, g + 1 - 2 * core)

    barrier = pltpu.get_barrier_semaphore()
    for who in (nxt, prv, xp, cp):
        pl.semaphore_signal(barrier, inc=1, device_id=who, device_id_type=MESH)

    load_y = pltpu.make_async_copy(y_hbm, y_ref, ls.at[0])
    load_x = pltpu.make_async_copy(x_hbm, x_ref, ls.at[1])
    load_y.start()
    load_x.start()

    def rows(slot, c):
        return pl.ds(pl.multiple_of(slot * R + c * C, 16), C)

    def copy(src, dst, ssem, rsem, who):
        return pltpu.make_async_remote_copy(
            src_ref=src, dst_ref=dst, send_sem=ssem, recv_sem=rsem, device_id=who, device_id_type=MESH
        )

    kinds = ((OWN, M1, nxt), (M1, M2, nxt), (M2, M3, nxt), (OWN, P1, prv), (P1, P2, prv))

    def piece(kind, c):
        src, dst, who = kinds[kind]
        return copy(ys.at[rows(src, c)], ys.at[rows(dst, c)], ysend.at[kind, c], yrecv.at[kind, c], who)

    def acc(kind, c):
        who = prv if kind < 3 else nxt
        return copy(accs.at[rows(kind, c)], accr.at[rows(kind, c)], asend.at[kind, c], arecv.at[kind, c], who)

    def block(k, count=1):
        return pl.ds(k * R, count * R)

    gather_x = copy(xf.at[block(0)], xf.at[block(1)], gs.at[0], gr.at[0], xp)
    gather_c = copy(xf.at[block(0)], xf.at[block(2)], gs.at[1], gr.at[1], cp)
    gather_d = copy(xf.at[block(1)], xf.at[block(3)], gs.at[2], gr.at[2], cp)
    reduce_c = copy(gsend, grecv, gs.at[3], gr.at[3], cp)
    reduce_x = copy(xsend, xrecv, gs.at[4], gr.at[4], xp)

    def loop(body):
        lax.fori_loop(0, N, lambda c, _: (body(c), 0)[1], 0)

    load_y.wait()
    wide = y_ref[...].astype(F32)
    ys[block(OWN)] = (wide * inv_norm(wide)).astype(BF16)
    load_x.wait()
    wide = x_ref[...].astype(F32)
    xf[block(0)] = (wide * inv_norm(wide)).astype(BF16)
    pl.semaphore_wait(barrier, 4)

    @loop
    def _(c):
        piece(0, c).start()
        piece(3, c).start()

    gather_x.start()
    gather_c.start()

    @loop
    def _(c):
        piece(0, c).wait_recv()
        piece(1, c).start()
        piece(3, c).wait_recv()
        piece(4, c).start()
    gather_x.wait_recv()
    gather_d.start()
    gather_c.wait_recv()
    gather_d.wait_recv()

    scale = s_ref[0]
    bias = b_ref[0]

    keep = {OWN: 0, M1: 1, M2: 2, P1: 3}
    send = {M3: 0, P2: 3}

    def task(slot, c, count):
        size = count * C
        spot = pl.ds(pl.multiple_of(slot * R + c * C, 16), size)
        y = ys[spot]
        dots = lax.dot_general(y, xf[...], (((1,), (1,)), ((), ())), preferred_element_type=F32)
        z = scale * dots + bias
        if slot == OWN:
            here = lax.broadcasted_iota(jnp.int32, (size, 4 * R), 1) == (
                lax.broadcasted_iota(jnp.int32, (size, 4 * R), 0) + c * C
            )
            sign = jnp.where(here, -1.0, 1.0).astype(F32)
            coef = sign * scale / (1.0 + jnp.exp(-sign * z))
        else:
            coef = scale / (1.0 + jnp.exp(-z))
        coef = coef.astype(BF16)
        ct[spot] = coef
        grad = jnp.dot(coef, xf[...], preferred_element_type=F32)
        if slot in keep:
            part[pl.ds(pl.multiple_of(keep[slot] * R + c * C, 16), size)] = grad
        else:
            accs[pl.ds(pl.multiple_of(send[slot] * R + c * C, 16), size)] = grad.astype(BF16)

    def forward(c):
        piece(1, c).wait_recv()
        piece(2, c).start()

    for c in range(N):
        forward(c)
        if c < 3:
            task((OWN, M1, P1)[c], 0, N)
    for slot in (OWN, M1, P1)[N:]:
        task(slot, 0, N)

    @loop
    def _(c):
        piece(4, c).wait_recv()

    task(P2, 0, N)
    task(M2, 0, N)

    def grads(lo, first, last):
        k = pl.ds(first * R, (last - first) * R)
        return lax.dot_general(
            ct[k, lo * R : (lo + 2) * R], ys[k], (((0,), (0,)), ((), ())), preferred_element_type=F32
        )

    gown[block(0, 2)] = grads(0, OWN, M3)
    gown[block(2, 2)] = grads(2, OWN, M3)

    def last_piece(q, _):
        for k in range(G):
            piece(2, q * G + k).wait_recv()
        task(M3, q * G, G)
        for k in range(G):
            acc(0, q * G + k).start()
            acc(3, q * G + k).start()
        return 0

    lax.fori_loop(0, N // G, last_piece, 0)

    gsend[...] = (gown[block(2, 2)] + grads(2, M3, M3 + 1)).astype(BF16)
    reduce_c.start()
    gown[block(0, 2)] += grads(0, M3, M3 + 1)
    reduce_c.wait_recv()
    xsend[...] = (gown[block(1)] + grecv[block(1)].astype(F32)).astype(BF16)
    reduce_x.start()

    def pass_on(src, mine, dst, c):
        acc(src, c).wait_recv()
        accs[rows(dst, c)] = (part[rows(mine, c)] + accr[rows(src, c)].astype(F32)).astype(BF16)
        acc(dst, c).start()

    @loop
    def _(c):
        pass_on(0, 2, 1, c)
        pass_on(3, 3, 4, c)

    @loop
    def _(c):
        pass_on(1, 1, 2, c)

    @loop
    def _(c):
        acc(4, c).wait_recv()
        acc(2, c).wait_recv()
        grad = part[rows(0, c)] + accr[rows(4, c)].astype(F32) + accr[rows(2, c)].astype(F32)
        gy_ref[rows(0, c)] = back_rows(y_ref[rows(0, c)], grad)

    reduce_x.wait_recv()
    total = gown[block(0)] + grecv[block(0)].astype(F32) + xrecv[...].astype(F32)
    gx_ref[...] = back_rows(x_ref[...], total)

    @loop
    def _(c):
        for kind in range(5):
            piece(kind, c).wait_send()
            acc(kind, c).wait_send()

    for one in (gather_x, gather_c, gather_d, reduce_c, reduce_x):
        one.wait_send()


def solution(mesh):
    nb = mesh.shape["blk"]

    def local(x, y, s, b):
        hbm = pl.BlockSpec(memory_space=pl.ANY)
        vmem = pl.BlockSpec(memory_space=pltpu.VMEM)
        smem = pl.BlockSpec(memory_space=pltpu.SMEM)
        dma = pltpu.SemaphoreType.DMA
        return pl.pallas_call(
            functools.partial(kernel, nb),
            out_shape=[jax.ShapeDtypeStruct((R, D), F32)] * 2,
            in_specs=[hbm, hbm, smem, smem],
            out_specs=[vmem, vmem],
            scratch_shapes=[
                pltpu.VMEM((R, D), BF16),
                pltpu.VMEM((R, D), BF16),
                pltpu.VMEM((4 * R, D), BF16),
                pltpu.VMEM((6 * R, D), BF16),
                pltpu.VMEM((6 * R, 4 * R), BF16),
                pltpu.VMEM((4 * R, D), F32),
                pltpu.VMEM((5 * R, D), BF16),
                pltpu.VMEM((5 * R, D), BF16),
                pltpu.VMEM((2 * R, D), BF16),
                pltpu.VMEM((2 * R, D), BF16),
                pltpu.VMEM((R, D), BF16),
                pltpu.VMEM((R, D), BF16),
                pltpu.VMEM((4 * R, D), F32),
                dma((5, N)),
                dma((5, N)),
                dma((5, N)),
                dma((5, N)),
                dma((5,)),
                dma((5,)),
                dma((2,)),
            ],
            compiler_params=pltpu.CompilerParams(
                collective_id=0, has_side_effects=True, vmem_limit_bytes=48 * 2**20
            ),
            cost_estimate=pl.CostEstimate(flops=4 * 10**9, bytes_accessed=2 * 10**6, transcendentals=10**6),
        )(x, y, s, b)

    spec = P(("blk", "grp"), None)
    return jax.shard_map(
        local, mesh=mesh, in_specs=(spec, spec, P(), P()), out_specs=(spec, spec), check_vma=False
    )
```

```python
import functools

import jax
import jax.numpy as jnp
from jax import lax
from jax.experimental import pallas as pl
from jax.experimental.pallas import tpu as pltpu
from jax.sharding import PartitionSpec as P

MESH = pl.DeviceIdType.MESH
R = 192
D = 768
RUN = 8
N = 4
G = 1
C = R // N
F32 = jnp.float32
BF16 = jnp.bfloat16

OWN, M1, P1, P2, M2, M3 = 0, 1, 2, 3, 4, 5


def inv_norm(wide):
    return lax.rsqrt(jnp.sum(wide * wide, axis=-1, keepdims=True) + 1e-06)


def back_rows(values, grad):
    wide = values.astype(F32)
    scale = inv_norm(wide)
    unit = wide * scale
    return scale * (grad - unit * jnp.sum(unit * grad, axis=-1, keepdims=True))


def kernel(
    nb, xy_ref, s_ref, b_ref, gx_ref, gy_ref,
    xf, xt, ys, ct, part, accs, accr, gsend, grecv, xsend, xrecv, gown,
    ysend, yrecv, asend, arecv, gs, gr,
):
    x_ref, y_ref = xy_ref.at[pl.ds(0, R)], xy_ref.at[pl.ds(R, R)]
    b = lax.axis_index("blk")
    g = lax.axis_index("grp")
    core = lax.rem(g, 2)
    spot = lax.rem(b, 2 * RUN)
    last = jnp.where(core == 0, 2 * RUN - 1, RUN - 1)
    first = jnp.where(core == 0, 0, RUN)
    partner = lax.rem(g + 2, 4)
    nxt = (lax.rem(b + 1, nb), jnp.where(spot == last, partner, g))
    prv = (lax.rem(b + nb - 1, nb), jnp.where(spot == first, partner, g))
    xp = (b, partner)
    cp = (b, g + 1 - 2 * core)

    barrier = pltpu.get_barrier_semaphore()
    for who in (nxt, prv, xp, cp):
        pl.semaphore_signal(barrier, inc=1, device_id=who, device_id_type=MESH)

    def rows(slot, c):
        return pl.ds(pl.multiple_of(slot * R + c * C, 16), C)

    def copy(src, dst, ssem, rsem, who):
        return pltpu.make_async_remote_copy(
            src_ref=src, dst_ref=dst, send_sem=ssem, recv_sem=rsem, device_id=who, device_id_type=MESH
        )

    kinds = ((OWN, M1, nxt), (M1, M2, nxt), (M2, M3, nxt), (OWN, P1, prv), (P1, P2, prv))

    def piece(kind, c):
        src, dst, who = kinds[kind]
        return copy(ys.at[rows(src, c)], ys.at[rows(dst, c)], ysend.at[kind, c], yrecv.at[kind, c], who)

    def acc(kind, c):
        who = prv if kind < 3 else nxt
        return copy(accs.at[rows(kind, c)], accr.at[rows(kind, c)], asend.at[kind, c], arecv.at[kind, c], who)

    def block(k, count=1):
        return pl.ds(k * R, count * R)

    gather_x = copy(xf.at[block(0)], xf.at[block(1)], gs.at[0], gr.at[0], xp)
    gather_c = copy(xf.at[block(0)], xf.at[block(2)], gs.at[1], gr.at[1], cp)
    gather_d = copy(xf.at[block(1)], xf.at[block(3)], gs.at[2], gr.at[2], cp)
    reduce_c = copy(gsend, grecv, gs.at[3], gr.at[3], cp)
    reduce_x = copy(xsend, xrecv, gs.at[4], gr.at[4], xp)

    def loop(body):
        lax.fori_loop(0, N, lambda c, _: (body(c), 0)[1], 0)

    wide = y_ref[...].astype(F32)
    ys[block(OWN)] = (wide * inv_norm(wide)).astype(BF16)
    wide = x_ref[...].astype(F32)
    xf[block(0)] = (wide * inv_norm(wide)).astype(BF16)
    pl.semaphore_wait(barrier, 4)

    @loop
    def _(c):
        piece(0, c).start()
        piece(3, c).start()

    gather_x.start()
    gather_c.start()

    @loop
    def _(c):
        piece(0, c).wait_recv()
        piece(1, c).start()
        piece(3, c).wait_recv()
        piece(4, c).start()
    gather_x.wait_recv()
    gather_d.start()
    gather_c.wait_recv()
    gather_d.wait_recv()
    xt[...] = xf[...].T

    scale = s_ref[0]
    bias = b_ref[0]

    keep = {OWN: 0, M1: 1, M2: 2, P1: 3}
    send = {M3: 0, P2: 3}

    def task(slot, c, count):
        size = count * C
        spot = pl.ds(pl.multiple_of(slot * R + c * C, 16), size)
        y = ys[spot]
        dots = jnp.dot(y, xt[...], preferred_element_type=F32)
        z = scale * dots + bias
        if slot == OWN:
            here = lax.broadcasted_iota(jnp.int32, (size, 4 * R), 1) == (
                lax.broadcasted_iota(jnp.int32, (size, 4 * R), 0) + c * C
            )
            sign = jnp.where(here, -1.0, 1.0).astype(F32)
            coef = sign * scale / (1.0 + jnp.exp(-sign * z))
        else:
            coef = scale / (1.0 + jnp.exp(-z))
        coef = coef.astype(BF16)
        ct[spot] = coef
        grad = jnp.dot(coef, xf[...], preferred_element_type=F32)
        if slot in keep:
            part[pl.ds(pl.multiple_of(keep[slot] * R + c * C, 16), size)] = grad
        else:
            accs[pl.ds(pl.multiple_of(send[slot] * R + c * C, 16), size)] = grad.astype(BF16)

    def forward(c):
        piece(1, c).wait_recv()
        piece(2, c).start()

    for c in range(N):
        forward(c)
        if c < 3:
            task((OWN, M1, P1)[c], 0, N)
    for slot in (OWN, M1, P1)[N:]:
        task(slot, 0, N)

    @loop
    def _(c):
        piece(4, c).wait_recv()

    task(P2, 0, N)
    task(M2, 0, N)

    def grads(lo, first, last):
        k = pl.ds(first * R, (last - first) * R)
        return lax.dot_general(
            ct[k, lo * R : (lo + 2) * R], ys[k], (((0,), (0,)), ((), ())), preferred_element_type=F32
        )

    gown[block(0, 2)] = grads(0, OWN, M3)
    gown[block(2, 2)] = grads(2, OWN, M3)

    def last_piece(q, _):
        for k in range(G):
            piece(2, q * G + k).wait_recv()
        task(M3, q * G, G)
        for k in range(G):
            acc(0, q * G + k).start()
            acc(3, q * G + k).start()
        return 0

    lax.fori_loop(0, N // G, last_piece, 0)

    gsend[...] = (gown[block(2, 2)] + grads(2, M3, M3 + 1)).astype(BF16)
    reduce_c.start()
    gown[block(0, 2)] += grads(0, M3, M3 + 1)
    reduce_c.wait_recv()
    xsend[...] = (gown[block(1)] + grecv[block(1)].astype(F32)).astype(BF16)
    reduce_x.start()

    def pass_on(src, mine, dst, c):
        acc(src, c).wait_recv()
        accs[rows(dst, c)] = (part[rows(mine, c)] + accr[rows(src, c)].astype(F32)).astype(BF16)
        acc(dst, c).start()

    @loop
    def _(c):
        pass_on(0, 2, 1, c)
        pass_on(3, 3, 4, c)

    @loop
    def _(c):
        pass_on(1, 1, 2, c)

    @loop
    def _(c):
        acc(4, c).wait_recv()
        acc(2, c).wait_recv()
        grad = part[rows(0, c)] + accr[rows(4, c)].astype(F32) + accr[rows(2, c)].astype(F32)
        gy_ref[rows(0, c)] = back_rows(y_ref[rows(0, c)], grad)

    reduce_x.wait_recv()
    total = gown[block(0)] + grecv[block(0)].astype(F32) + xrecv[...].astype(F32)
    gx_ref[...] = back_rows(x_ref[...], total)

    @loop
    def _(c):
        for kind in range(5):
            piece(kind, c).wait_send()
            acc(kind, c).wait_send()

    for one in (gather_x, gather_c, gather_d, reduce_c, reduce_x):
        one.wait_send()


def store(gx_ref, gy_ref, gx_hbm, gy_hbm, sems):
    copies = [
        pltpu.make_async_copy(gx_ref, gx_hbm, sems.at[0]),
        pltpu.make_async_copy(gy_ref, gy_hbm, sems.at[1]),
    ]
    for one in copies:
        one.start()
    for one in copies:
        one.wait()


def solution(mesh):
    nb = mesh.shape["blk"]

    def local(x, y, s, b):
        hbm = pl.BlockSpec(memory_space=pl.ANY)
        vmem = pl.BlockSpec(memory_space=pltpu.VMEM)
        smem = pl.BlockSpec(memory_space=pltpu.SMEM)
        dma = pltpu.SemaphoreType.DMA
        rows = jnp.concatenate([x, y])
        grads = pl.pallas_call(
            functools.partial(kernel, nb),
            out_shape=[jax.ShapeDtypeStruct((R, D), F32)] * 2,
            in_specs=[vmem, smem, smem],
            out_specs=[vmem, vmem],
            scratch_shapes=[
                pltpu.VMEM((4 * R, D), BF16),
                pltpu.VMEM((4 * R, D), BF16),
                pltpu.VMEM((6 * R, D), BF16),
                pltpu.VMEM((6 * R, 4 * R), BF16),
                pltpu.VMEM((4 * R, D), F32),
                pltpu.VMEM((5 * R, D), BF16),
                pltpu.VMEM((5 * R, D), BF16),
                pltpu.VMEM((2 * R, D), BF16),
                pltpu.VMEM((2 * R, D), BF16),
                pltpu.VMEM((R, D), BF16),
                pltpu.VMEM((R, D), BF16),
                pltpu.VMEM((4 * R, D), F32),
                dma((5, N)),
                dma((5, N)),
                dma((5, N)),
                dma((5, N)),
                dma((5,)),
                dma((5,)),
            ],
            compiler_params=pltpu.CompilerParams(
                collective_id=0, has_side_effects=True, vmem_limit_bytes=48 * 2**20
            ),
            cost_estimate=pl.CostEstimate(flops=4 * 10**9, bytes_accessed=2 * 10**6, transcendentals=10**6),
        )(rows, s, b)
        return pl.pallas_call(
            store,
            out_shape=[jax.ShapeDtypeStruct((R, D), F32)] * 2,
            in_specs=[vmem, vmem],
            out_specs=[hbm, hbm],
            scratch_shapes=[dma((2,))],
            compiler_params=pltpu.CompilerParams(vmem_limit_bytes=4 * 2**20),
        )(*grads)

    spec = P(("blk", "grp"), None)
    return jax.shard_map(
        local, mesh=mesh, in_specs=(spec, spec, P(), P()), out_specs=(spec, spec), check_vma=False
    )
```

```python
import functools

import jax
import jax.numpy as jnp
from jax import lax
from jax.experimental import pallas as pl
from jax.experimental.pallas import tpu as pltpu
from jax.sharding import PartitionSpec as P

MESH = pl.DeviceIdType.MESH
R = 192
D = 768
RUN = 8
N = 4
G = 1
C = R // N
F32 = jnp.float32
BF16 = jnp.bfloat16

OWN, M1, P1, P2, M2, M3 = 0, 1, 2, 3, 4, 5


def inv_norm(wide):
    return lax.rsqrt(jnp.sum(wide * wide, axis=-1, keepdims=True) + 1e-06)


def back_rows(values, grad):
    wide = values.astype(F32)
    scale = inv_norm(wide)
    unit = wide * scale
    return scale * (grad - unit * jnp.sum(unit * grad, axis=-1, keepdims=True))


def kernel(
    nb, xy_ref, s_ref, b_ref, gx_ref, gy_ref,
    xf, xt, ys, ct, part, accs, accr, gsend, grecv, xsend, xrecv, gown,
    ysend, yrecv, asend, arecv, gs, gr,
):
    x_ref, y_ref = xy_ref.at[pl.ds(0, R)], xy_ref.at[pl.ds(R, R)]
    b = lax.axis_index("blk")
    g = lax.axis_index("grp")
    core = lax.rem(g, 2)
    spot = lax.rem(b, 2 * RUN)
    last = jnp.where(core == 0, 2 * RUN - 1, RUN - 1)
    first = jnp.where(core == 0, 0, RUN)
    partner = lax.rem(g + 2, 4)
    nxt = (lax.rem(b + 1, nb), jnp.where(spot == last, partner, g))
    prv = (lax.rem(b + nb - 1, nb), jnp.where(spot == first, partner, g))
    xp = (b, partner)
    cp = (b, g + 1 - 2 * core)

    barrier = pltpu.get_barrier_semaphore()
    for who in (xp, nxt, prv, cp):
        pl.semaphore_signal(barrier, inc=1, device_id=who, device_id_type=MESH)

    def rows(slot, c):
        return pl.ds(pl.multiple_of(slot * R + c * C, 16), C)

    def copy(src, dst, ssem, rsem, who):
        return pltpu.make_async_remote_copy(
            src_ref=src, dst_ref=dst, send_sem=ssem, recv_sem=rsem, device_id=who, device_id_type=MESH
        )

    kinds = ((OWN, M1, nxt), (M1, M2, nxt), (M2, M3, nxt), (OWN, P1, prv), (P1, P2, prv))

    def piece(kind, c):
        src, dst, who = kinds[kind]
        return copy(ys.at[rows(src, c)], ys.at[rows(dst, c)], ysend.at[kind, c], yrecv.at[kind, c], who)

    def acc(kind, c):
        who = prv if kind < 3 else nxt
        return copy(accs.at[rows(kind, c)], accr.at[rows(kind, c)], asend.at[kind, c], arecv.at[kind, c], who)

    def block(k, count=1):
        return pl.ds(k * R, count * R)

    gather_x = copy(xf.at[block(0)], xf.at[block(1)], gs.at[0], gr.at[0], xp)
    gather_c = copy(xf.at[block(0)], xf.at[block(2)], gs.at[1], gr.at[1], cp)
    gather_d = copy(xf.at[block(1)], xf.at[block(3)], gs.at[2], gr.at[2], cp)
    reduce_c = copy(gsend, grecv, gs.at[3], gr.at[3], cp)
    reduce_x = copy(xsend, xrecv, gs.at[4], gr.at[4], xp)

    def loop(body):
        lax.fori_loop(0, N, lambda c, _: (body(c), 0)[1], 0)

    wide = y_ref[...].astype(F32)
    ys[block(OWN)] = (wide * inv_norm(wide)).astype(BF16)
    wide = x_ref[...].astype(F32)
    xf[block(0)] = (wide * inv_norm(wide)).astype(BF16)
    pl.semaphore_wait(barrier, 4)

    @loop
    def _(c):
        piece(0, c).start()
        piece(3, c).start()

    gather_x.start()
    gather_c.start()

    @loop
    def _(c):
        piece(0, c).wait_recv()
        piece(1, c).start()
        piece(3, c).wait_recv()
        piece(4, c).start()
    gather_x.wait_recv()
    gather_d.start()
    gather_c.wait_recv()
    gather_d.wait_recv()
    xt[...] = xf[...].T

    scale = s_ref[0]
    bias = b_ref[0]

    keep = {OWN: 0, M1: 1, M2: 2, P1: 3}
    send = {M3: 0, P2: 3}

    def task(slot, c, count):
        size = count * C
        spot = pl.ds(pl.multiple_of(slot * R + c * C, 16), size)
        y = ys[spot]
        dots = jnp.dot(y, xt[...], preferred_element_type=F32)
        z = scale * dots + bias
        if slot == OWN:
            here = lax.broadcasted_iota(jnp.int32, (size, 4 * R), 1) == (
                lax.broadcasted_iota(jnp.int32, (size, 4 * R), 0) + c * C
            )
            sign = jnp.where(here, -1.0, 1.0).astype(F32)
            coef = sign * scale / (1.0 + jnp.exp(-sign * z))
        else:
            coef = scale / (1.0 + jnp.exp(-z))
        coef = coef.astype(BF16)
        ct[spot] = coef
        grad = jnp.dot(coef, xf[...], preferred_element_type=F32)
        if slot in keep:
            part[pl.ds(pl.multiple_of(keep[slot] * R + c * C, 16), size)] = grad
        else:
            accs[pl.ds(pl.multiple_of(send[slot] * R + c * C, 16), size)] = grad.astype(BF16)

    def forward(c):
        piece(1, c).wait_recv()
        piece(2, c).start()

    for c in range(N):
        forward(c)
        if c < 3:
            task((OWN, M1, P1)[c], 0, N)
    for slot in (OWN, M1, P1)[N:]:
        task(slot, 0, N)

    @loop
    def _(c):
        piece(4, c).wait_recv()

    task(P2, 0, N)
    task(M2, 0, N)

    def grads(lo, first, last):
        k = pl.ds(first * R, (last - first) * R)
        return lax.dot_general(
            ct[k, lo * R : (lo + 2) * R], ys[k], (((0,), (0,)), ((), ())), preferred_element_type=F32
        )

    gown[block(0, 2)] = grads(0, OWN, M3)
    gown[block(2, 2)] = grads(2, OWN, M3)

    def last_piece(q, _):
        for k in range(G):
            piece(2, q * G + k).wait_recv()
        task(M3, q * G, G)
        for k in range(G):
            acc(0, q * G + k).start()
            acc(3, q * G + k).start()
        return 0

    lax.fori_loop(0, N // G, last_piece, 0)

    gsend[...] = (gown[block(2, 2)] + grads(2, M3, M3 + 1)).astype(BF16)
    reduce_c.start()
    gown[block(0, 2)] += grads(0, M3, M3 + 1)
    reduce_c.wait_recv()
    xsend[...] = (gown[block(1)] + grecv[block(1)].astype(F32)).astype(BF16)
    reduce_x.start()

    def pass_on(src, mine, dst, c):
        acc(src, c).wait_recv()
        accs[rows(dst, c)] = (part[rows(mine, c)] + accr[rows(src, c)].astype(F32)).astype(BF16)
        acc(dst, c).start()

    @loop
    def _(c):
        pass_on(0, 2, 1, c)
        pass_on(3, 3, 4, c)

    @loop
    def _(c):
        pass_on(1, 1, 2, c)

    reduce_x.wait_recv()
    total = gown[block(0)] + grecv[block(0)].astype(F32) + xrecv[...].astype(F32)
    gx_ref[...] = back_rows(x_ref[...], total)

    @loop
    def _(c):
        acc(4, c).wait_recv()
        acc(2, c).wait_recv()
        grad = part[rows(0, c)] + accr[rows(4, c)].astype(F32) + accr[rows(2, c)].astype(F32)
        gy_ref[rows(0, c)] = back_rows(y_ref[rows(0, c)], grad)

    @loop
    def _(c):
        for kind in range(5):
            piece(kind, c).wait_send()
            acc(kind, c).wait_send()

    for one in (gather_x, gather_c, gather_d, reduce_c, reduce_x):
        one.wait_send()


def store(gx_ref, gy_ref, gx_hbm, gy_hbm, sems):
    copies = [
        pltpu.make_async_copy(gx_ref, gx_hbm, sems.at[0]),
        pltpu.make_async_copy(gy_ref, gy_hbm, sems.at[1]),
    ]
    for one in copies:
        one.start()
    for one in copies:
        one.wait()


def solution(mesh):
    nb = mesh.shape["blk"]

    def local(x, y, s, b):
        hbm = pl.BlockSpec(memory_space=pl.ANY)
        vmem = pl.BlockSpec(memory_space=pltpu.VMEM)
        smem = pl.BlockSpec(memory_space=pltpu.SMEM)
        dma = pltpu.SemaphoreType.DMA
        rows = jnp.concatenate([x, y])
        grads = pl.pallas_call(
            functools.partial(kernel, nb),
            out_shape=[jax.ShapeDtypeStruct((R, D), F32)] * 2,
            in_specs=[vmem, smem, smem],
            out_specs=[vmem, vmem],
            scratch_shapes=[
                pltpu.VMEM((4 * R, D), BF16),
                pltpu.VMEM((4 * R, D), BF16),
                pltpu.VMEM((6 * R, D), BF16),
                pltpu.VMEM((6 * R, 4 * R), BF16),
                pltpu.VMEM((4 * R, D), F32),
                pltpu.VMEM((5 * R, D), BF16),
                pltpu.VMEM((5 * R, D), BF16),
                pltpu.VMEM((2 * R, D), BF16),
                pltpu.VMEM((2 * R, D), BF16),
                pltpu.VMEM((R, D), BF16),
                pltpu.VMEM((R, D), BF16),
                pltpu.VMEM((4 * R, D), F32),
                dma((5, N)),
                dma((5, N)),
                dma((5, N)),
                dma((5, N)),
                dma((5,)),
                dma((5,)),
            ],
            compiler_params=pltpu.CompilerParams(
                collective_id=0, has_side_effects=True, vmem_limit_bytes=48 * 2**20
            ),
            cost_estimate=pl.CostEstimate(flops=4 * 10**9, bytes_accessed=2 * 10**6, transcendentals=10**6),
        )(rows, s, b)
        return pl.pallas_call(
            store,
            out_shape=[jax.ShapeDtypeStruct((R, D), F32)] * 2,
            in_specs=[vmem, vmem],
            out_specs=[hbm, hbm],
            scratch_shapes=[dma((2,))],
            compiler_params=pltpu.CompilerParams(vmem_limit_bytes=4 * 2**20),
        )(*grads)

    spec = P(("blk", "grp"), None)
    return jax.shard_map(
        local, mesh=mesh, in_specs=(spec, spec, P(), P()), out_specs=(spec, spec), check_vma=False
    )
```

```python
import functools

import jax
import jax.numpy as jnp
from jax import lax
from jax.experimental import pallas as pl
from jax.experimental.pallas import tpu as pltpu
from jax.sharding import PartitionSpec as P

MESH = pl.DeviceIdType.MESH
R = 192
D = 768
RUN = 8
N = 4
G = 1
C = R // N
F32 = jnp.float32
BF16 = jnp.bfloat16

OWN, M1, P1, P2, M2, M3 = 0, 1, 2, 3, 4, 5


def inv_norm(wide):
    return lax.rsqrt(jnp.sum(wide * wide, axis=-1, keepdims=True) + 1e-06)


def back_rows(values, grad):
    wide = values.astype(F32)
    scale = inv_norm(wide)
    unit = wide * scale
    return scale * (grad - unit * jnp.sum(unit * grad, axis=-1, keepdims=True))


def kernel(
    nb, xy_ref, s_ref, b_ref, gx_ref, gy_ref,
    xf, xt, ys, ct, part, accs, accr, gsend, grecv, xsend, xrecv, gown,
    ysend, yrecv, asend, arecv, gs, gr,
):
    x_ref, y_ref = xy_ref.at[pl.ds(0, R)], xy_ref.at[pl.ds(R, R)]
    b = lax.axis_index("blk")
    g = lax.axis_index("grp")
    core = lax.rem(g, 2)
    spot = lax.rem(b, 2 * RUN)
    last = jnp.where(core == 0, 2 * RUN - 1, RUN - 1)
    first = jnp.where(core == 0, 0, RUN)
    partner = lax.rem(g + 2, 4)
    nxt = (lax.rem(b + 1, nb), jnp.where(spot == last, partner, g))
    prv = (lax.rem(b + nb - 1, nb), jnp.where(spot == first, partner, g))
    xp = (b, partner)
    cp = (b, g + 1 - 2 * core)

    barrier = pltpu.get_barrier_semaphore()
    for who in (xp, nxt, prv, cp):
        pl.semaphore_signal(barrier, inc=1, device_id=who, device_id_type=MESH)

    def rows(slot, c):
        return pl.ds(pl.multiple_of(slot * R + c * C, 16), C)

    def copy(src, dst, ssem, rsem, who):
        return pltpu.make_async_remote_copy(
            src_ref=src, dst_ref=dst, send_sem=ssem, recv_sem=rsem, device_id=who, device_id_type=MESH
        )

    kinds = ((OWN, M1, nxt), (M1, M2, nxt), (M2, M3, nxt), (OWN, P1, prv), (P1, P2, prv))

    def piece(kind, c):
        src, dst, who = kinds[kind]
        return copy(ys.at[rows(src, c)], ys.at[rows(dst, c)], ysend.at[kind, c], yrecv.at[kind, c], who)

    def acc(kind, c):
        who = prv if kind < 3 else nxt
        return copy(accs.at[rows(kind, c)], accr.at[rows(kind, c)], asend.at[kind, c], arecv.at[kind, c], who)

    def block(k, count=1):
        return pl.ds(k * R, count * R)

    gather_x = copy(xf.at[block(0)], xf.at[block(1)], gs.at[0], gr.at[0], xp)
    gather_c = copy(xf.at[block(0)], xf.at[block(2)], gs.at[1], gr.at[1], cp)
    gather_d = copy(xf.at[block(1)], xf.at[block(3)], gs.at[2], gr.at[2], cp)
    reduce_c = copy(gsend, grecv, gs.at[3], gr.at[3], cp)
    reduce_x = copy(xsend, xrecv, gs.at[4], gr.at[4], xp)

    def loop(body):
        lax.fori_loop(0, N, lambda c, _: (body(c), 0)[1], 0)

    wide = y_ref[...].astype(F32)
    ys[block(OWN)] = (wide * inv_norm(wide)).astype(BF16)
    wide = x_ref[...].astype(F32)
    xf[block(0)] = (wide * inv_norm(wide)).astype(BF16)
    pl.semaphore_wait(barrier, 4)

    @loop
    def _(c):
        piece(0, c).start()
        piece(3, c).start()

    gather_x.start()
    gather_c.start()

    @loop
    def _(c):
        piece(0, c).wait_recv()
        piece(1, c).start()
        piece(3, c).wait_recv()
        piece(4, c).start()

    def forward(c):
        piece(1, c).wait_recv()
        piece(2, c).start()

    gather_x.wait_recv()
    gather_d.start()
    forward(0)
    gather_c.wait_recv()
    gather_d.wait_recv()
    xt[...] = xf[...].T

    scale = s_ref[0]
    bias = b_ref[0]

    keep = {OWN: 0, M1: 1, M2: 2, P1: 3}
    send = {M3: 0, P2: 3}

    def task(slot, c, count):
        size = count * C
        spot = pl.ds(pl.multiple_of(slot * R + c * C, 16), size)
        y = ys[spot]
        dots = jnp.dot(y, xt[...], preferred_element_type=F32)
        z = scale * dots + bias
        if slot == OWN:
            here = lax.broadcasted_iota(jnp.int32, (size, 4 * R), 1) == (
                lax.broadcasted_iota(jnp.int32, (size, 4 * R), 0) + c * C
            )
            sign = jnp.where(here, -1.0, 1.0).astype(F32)
            coef = sign * scale / (1.0 + jnp.exp(-sign * z))
        else:
            coef = scale / (1.0 + jnp.exp(-z))
        coef = coef.astype(BF16)
        ct[spot] = coef
        grad = jnp.dot(coef, xf[...], preferred_element_type=F32)
        if slot in keep:
            part[pl.ds(pl.multiple_of(keep[slot] * R + c * C, 16), size)] = grad
        else:
            accs[pl.ds(pl.multiple_of(send[slot] * R + c * C, 16), size)] = grad.astype(BF16)

    for c in range(N):
        if c > 0:
            forward(c)
        if c < 3:
            task((OWN, M1, P1)[c], 0, N)
    for slot in (OWN, M1, P1)[N:]:
        task(slot, 0, N)

    @loop
    def _(c):
        piece(4, c).wait_recv()

    task(P2, 0, N)
    task(M2, 0, N)

    def grads(lo, first, last):
        k = pl.ds(first * R, (last - first) * R)
        return lax.dot_general(
            ct[k, lo * R : (lo + 2) * R], ys[k], (((0,), (0,)), ((), ())), preferred_element_type=F32
        )

    gown[block(0, 2)] = grads(0, OWN, M3)
    gown[block(2, 2)] = grads(2, OWN, M3)

    def last_piece(q, _):
        for k in range(G):
            piece(2, q * G + k).wait_recv()
        task(M3, q * G, G)
        for k in range(G):
            acc(0, q * G + k).start()
            acc(3, q * G + k).start()
        return 0

    lax.fori_loop(0, N // G, last_piece, 0)

    gsend[...] = (gown[block(2, 2)] + grads(2, M3, M3 + 1)).astype(BF16)
    reduce_c.start()
    gown[block(0, 2)] += grads(0, M3, M3 + 1)
    reduce_c.wait_recv()
    xsend[...] = (gown[block(1)] + grecv[block(1)].astype(F32)).astype(BF16)
    reduce_x.start()

    def pass_on(src, mine, dst, c):
        acc(src, c).wait_recv()
        accs[rows(dst, c)] = (part[rows(mine, c)] + accr[rows(src, c)].astype(F32)).astype(BF16)
        acc(dst, c).start()

    @loop
    def _(c):
        pass_on(0, 2, 1, c)
        pass_on(3, 3, 4, c)

    @loop
    def _(c):
        pass_on(1, 1, 2, c)

    reduce_x.wait_recv()
    total = gown[block(0)] + grecv[block(0)].astype(F32) + xrecv[...].astype(F32)
    gx_ref[...] = back_rows(x_ref[...], total)

    @loop
    def _(c):
        acc(4, c).wait_recv()
        acc(2, c).wait_recv()
        grad = part[rows(0, c)] + accr[rows(4, c)].astype(F32) + accr[rows(2, c)].astype(F32)
        gy_ref[rows(0, c)] = back_rows(y_ref[rows(0, c)], grad)

    @loop
    def _(c):
        for kind in range(5):
            piece(kind, c).wait_send()
            acc(kind, c).wait_send()

    for one in (gather_x, gather_c, gather_d, reduce_c, reduce_x):
        one.wait_send()


def store(gx_ref, gy_ref, gx_hbm, gy_hbm, sems):
    copies = [
        pltpu.make_async_copy(gx_ref, gx_hbm, sems.at[0]),
        pltpu.make_async_copy(gy_ref, gy_hbm, sems.at[1]),
    ]
    for one in copies:
        one.start()
    for one in copies:
        one.wait()


def solution(mesh):
    nb = mesh.shape["blk"]

    def local(x, y, s, b):
        hbm = pl.BlockSpec(memory_space=pl.ANY)
        vmem = pl.BlockSpec(memory_space=pltpu.VMEM)
        smem = pl.BlockSpec(memory_space=pltpu.SMEM)
        dma = pltpu.SemaphoreType.DMA
        rows = jnp.concatenate([x, y])
        grads = pl.pallas_call(
            functools.partial(kernel, nb),
            out_shape=[jax.ShapeDtypeStruct((R, D), F32)] * 2,
            in_specs=[vmem, smem, smem],
            out_specs=[vmem, vmem],
            scratch_shapes=[
                pltpu.VMEM((4 * R, D), BF16),
                pltpu.VMEM((4 * R, D), BF16),
                pltpu.VMEM((6 * R, D), BF16),
                pltpu.VMEM((6 * R, 4 * R), BF16),
                pltpu.VMEM((4 * R, D), F32),
                pltpu.VMEM((5 * R, D), BF16),
                pltpu.VMEM((5 * R, D), BF16),
                pltpu.VMEM((2 * R, D), BF16),
                pltpu.VMEM((2 * R, D), BF16),
                pltpu.VMEM((R, D), BF16),
                pltpu.VMEM((R, D), BF16),
                pltpu.VMEM((4 * R, D), F32),
                dma((5, N)),
                dma((5, N)),
                dma((5, N)),
                dma((5, N)),
                dma((5,)),
                dma((5,)),
            ],
            compiler_params=pltpu.CompilerParams(
                collective_id=0, has_side_effects=True, vmem_limit_bytes=48 * 2**20
            ),
            cost_estimate=pl.CostEstimate(flops=4 * 10**9, bytes_accessed=2 * 10**6, transcendentals=10**6),
        )(rows, s, b)
        return pl.pallas_call(
            store,
            out_shape=[jax.ShapeDtypeStruct((R, D), F32)] * 2,
            in_specs=[vmem, vmem],
            out_specs=[hbm, hbm],
            scratch_shapes=[dma((2,))],
            compiler_params=pltpu.CompilerParams(vmem_limit_bytes=4 * 2**20),
        )(*grads)

    spec = P(("blk", "grp"), None)
    return jax.shard_map(
        local, mesh=mesh, in_specs=(spec, spec, P(), P()), out_specs=(spec, spec), check_vma=False
    )
```

```python
import functools

import jax
import jax.numpy as jnp
from jax import lax
from jax.experimental import pallas as pl
from jax.experimental.pallas import tpu as pltpu
from jax.sharding import PartitionSpec as P

MESH = pl.DeviceIdType.MESH
R = 192
D = 768
RUN = 8
N = 4
G = 1
C = R // N
F32 = jnp.float32
BF16 = jnp.bfloat16

OWN, M1, P1, P2, M2, M3 = 0, 1, 2, 3, 4, 5


def inv_norm(wide):
    return lax.rsqrt(jnp.sum(wide * wide, axis=-1, keepdims=True) + 1e-06)


def back_rows(values, grad):
    wide = values.astype(F32)
    scale = inv_norm(wide)
    unit = wide * scale
    return scale * (grad - unit * jnp.sum(unit * grad, axis=-1, keepdims=True))


def kernel(
    nb, xy_ref, s_ref, b_ref, gx_ref, gy_ref,
    xf, xt, ys, ct, part, accs, accr, gsend, grecv, xsend, xrecv, gown,
    ysend, yrecv, asend, arecv, gs, gr,
):
    x_ref, y_ref = xy_ref.at[pl.ds(0, R)], xy_ref.at[pl.ds(R, R)]
    b = lax.axis_index("blk")
    g = lax.axis_index("grp")
    core = lax.rem(g, 2)
    spot = lax.rem(b, 2 * RUN)
    last = jnp.where(core == 0, 2 * RUN - 1, RUN - 1)
    first = jnp.where(core == 0, 0, RUN)
    partner = lax.rem(g + 2, 4)
    nxt = (lax.rem(b + 1, nb), jnp.where(spot == last, partner, g))
    prv = (lax.rem(b + nb - 1, nb), jnp.where(spot == first, partner, g))
    xp = (b, partner)
    cp = (b, g + 1 - 2 * core)

    barrier = pltpu.get_barrier_semaphore()
    for who in (xp, nxt, prv, cp):
        pl.semaphore_signal(barrier, inc=1, device_id=who, device_id_type=MESH)

    def rows(slot, c):
        return pl.ds(pl.multiple_of(slot * R + c * C, 16), C)

    def copy(src, dst, ssem, rsem, who):
        return pltpu.make_async_remote_copy(
            src_ref=src, dst_ref=dst, send_sem=ssem, recv_sem=rsem, device_id=who, device_id_type=MESH
        )

    kinds = ((OWN, M1, nxt), (M1, M2, nxt), (M2, M3, nxt), (OWN, P1, prv), (P1, P2, prv))

    def piece(kind, c):
        src, dst, who = kinds[kind]
        return copy(ys.at[rows(src, c)], ys.at[rows(dst, c)], ysend.at[kind, c], yrecv.at[kind, c], who)

    def acc(kind, c):
        who = prv if kind < 3 else nxt
        return copy(accs.at[rows(kind, c)], accr.at[rows(kind, c)], asend.at[kind, c], arecv.at[kind, c], who)

    def block(k, count=1):
        return pl.ds(k * R, count * R)

    gather_x = copy(xf.at[block(0)], xf.at[block(1)], gs.at[0], gr.at[0], xp)
    gather_c = copy(xf.at[block(0)], xf.at[block(2)], gs.at[1], gr.at[1], cp)
    gather_d = copy(xf.at[block(1)], xf.at[block(3)], gs.at[2], gr.at[2], cp)
    reduce_c = copy(gsend, grecv, gs.at[3], gr.at[3], cp)
    reduce_x = copy(xsend, xrecv, gs.at[4], gr.at[4], xp)

    def loop(body):
        lax.fori_loop(0, N, lambda c, _: (body(c), 0)[1], 0)

    wide = y_ref[...].astype(F32)
    ys[block(OWN)] = (wide * inv_norm(wide)).astype(BF16)
    wide = x_ref[...].astype(F32)
    xf[block(0)] = (wide * inv_norm(wide)).astype(BF16)
    pl.semaphore_wait(barrier, 4)

    @loop
    def _(c):
        piece(0, c).start()
        piece(3, c).start()

    gather_x.start()
    gather_c.start()

    @loop
    def _(c):
        piece(0, c).wait_recv()
        piece(1, c).start()
        piece(3, c).wait_recv()
        piece(4, c).start()

    def forward(c):
        piece(1, c).wait_recv()
        piece(2, c).start()

    gather_x.wait_recv()
    gather_d.start()
    forward(0)
    gather_c.wait_recv()
    gather_d.wait_recv()
    forward(1)
    xt[...] = xf[...].T

    scale = s_ref[0]
    bias = b_ref[0]

    keep = {OWN: 0, M1: 1, M2: 2, P1: 3}
    send = {M3: 0, P2: 3}

    def task(slot, c, count):
        size = count * C
        spot = pl.ds(pl.multiple_of(slot * R + c * C, 16), size)
        y = ys[spot]
        dots = jnp.dot(y, xt[...], preferred_element_type=F32)
        z = scale * dots + bias
        if slot == OWN:
            here = lax.broadcasted_iota(jnp.int32, (size, 4 * R), 1) == (
                lax.broadcasted_iota(jnp.int32, (size, 4 * R), 0) + c * C
            )
            sign = jnp.where(here, -1.0, 1.0).astype(F32)
            coef = sign * scale / (1.0 + jnp.exp(-sign * z))
        else:
            coef = scale / (1.0 + jnp.exp(-z))
        coef = coef.astype(BF16)
        ct[spot] = coef
        grad = jnp.dot(coef, xf[...], preferred_element_type=F32)
        if slot in keep:
            part[pl.ds(pl.multiple_of(keep[slot] * R + c * C, 16), size)] = grad
        else:
            accs[pl.ds(pl.multiple_of(send[slot] * R + c * C, 16), size)] = grad.astype(BF16)

    for c in range(N):
        if c > 1:
            forward(c)
        if c < 3:
            task((OWN, M1, P1)[c], 0, N)
    for slot in (OWN, M1, P1)[N:]:
        task(slot, 0, N)

    @loop
    def _(c):
        piece(4, c).wait_recv()

    task(P2, 0, N)
    task(M2, 0, N)

    def grads(lo, first, last):
        k = pl.ds(first * R, (last - first) * R)
        return lax.dot_general(
            ct[k, lo * R : (lo + 2) * R], ys[k], (((0,), (0,)), ((), ())), preferred_element_type=F32
        )

    gown[block(0, 2)] = grads(0, OWN, M3)
    gown[block(2, 2)] = grads(2, OWN, M3)

    def last_piece(q, _):
        for k in range(G):
            piece(2, q * G + k).wait_recv()
        task(M3, q * G, G)
        for k in range(G):
            acc(0, q * G + k).start()
            acc(3, q * G + k).start()
        return 0

    lax.fori_loop(0, N // G, last_piece, 0)

    gsend[...] = (gown[block(2, 2)] + grads(2, M3, M3 + 1)).astype(BF16)
    reduce_c.start()
    gown[block(0, 2)] += grads(0, M3, M3 + 1)
    reduce_c.wait_recv()
    xsend[...] = (gown[block(1)] + grecv[block(1)].astype(F32)).astype(BF16)
    reduce_x.start()

    def pass_on(src, mine, dst, c):
        acc(src, c).wait_recv()
        accs[rows(dst, c)] = (part[rows(mine, c)] + accr[rows(src, c)].astype(F32)).astype(BF16)
        acc(dst, c).start()

    @loop
    def _(c):
        pass_on(0, 2, 1, c)
        pass_on(3, 3, 4, c)

    @loop
    def _(c):
        pass_on(1, 1, 2, c)

    reduce_x.wait_recv()
    total = gown[block(0)] + grecv[block(0)].astype(F32) + xrecv[...].astype(F32)
    gx_ref[...] = back_rows(x_ref[...], total)

    @loop
    def _(c):
        acc(4, c).wait_recv()
        acc(2, c).wait_recv()
        grad = part[rows(0, c)] + accr[rows(4, c)].astype(F32) + accr[rows(2, c)].astype(F32)
        gy_ref[rows(0, c)] = back_rows(y_ref[rows(0, c)], grad)

    @loop
    def _(c):
        for kind in range(5):
            piece(kind, c).wait_send()
            acc(kind, c).wait_send()

    for one in (gather_x, gather_c, gather_d, reduce_c, reduce_x):
        one.wait_send()


def store(gx_ref, gy_ref, gx_hbm, gy_hbm, sems):
    copies = [
        pltpu.make_async_copy(gx_ref, gx_hbm, sems.at[0]),
        pltpu.make_async_copy(gy_ref, gy_hbm, sems.at[1]),
    ]
    for one in copies:
        one.start()
    for one in copies:
        one.wait()


def solution(mesh):
    nb = mesh.shape["blk"]

    def local(x, y, s, b):
        hbm = pl.BlockSpec(memory_space=pl.ANY)
        vmem = pl.BlockSpec(memory_space=pltpu.VMEM)
        smem = pl.BlockSpec(memory_space=pltpu.SMEM)
        dma = pltpu.SemaphoreType.DMA
        rows = jnp.concatenate([x, y])
        grads = pl.pallas_call(
            functools.partial(kernel, nb),
            out_shape=[jax.ShapeDtypeStruct((R, D), F32)] * 2,
            in_specs=[vmem, smem, smem],
            out_specs=[vmem, vmem],
            scratch_shapes=[
                pltpu.VMEM((4 * R, D), BF16),
                pltpu.VMEM((4 * R, D), BF16),
                pltpu.VMEM((6 * R, D), BF16),
                pltpu.VMEM((6 * R, 4 * R), BF16),
                pltpu.VMEM((4 * R, D), F32),
                pltpu.VMEM((5 * R, D), BF16),
                pltpu.VMEM((5 * R, D), BF16),
                pltpu.VMEM((2 * R, D), BF16),
                pltpu.VMEM((2 * R, D), BF16),
                pltpu.VMEM((R, D), BF16),
                pltpu.VMEM((R, D), BF16),
                pltpu.VMEM((4 * R, D), F32),
                dma((5, N)),
                dma((5, N)),
                dma((5, N)),
                dma((5, N)),
                dma((5,)),
                dma((5,)),
            ],
            compiler_params=pltpu.CompilerParams(
                collective_id=0, has_side_effects=True, vmem_limit_bytes=48 * 2**20
            ),
            cost_estimate=pl.CostEstimate(flops=4 * 10**9, bytes_accessed=2 * 10**6, transcendentals=10**6),
        )(rows, s, b)
        return pl.pallas_call(
            store,
            out_shape=[jax.ShapeDtypeStruct((R, D), F32)] * 2,
            in_specs=[vmem, vmem],
            out_specs=[hbm, hbm],
            scratch_shapes=[dma((2,))],
            compiler_params=pltpu.CompilerParams(vmem_limit_bytes=4 * 2**20),
        )(*grads)

    spec = P(("blk", "grp"), None)
    return jax.shard_map(
        local, mesh=mesh, in_specs=(spec, spec, P(), P()), out_specs=(spec, spec), check_vma=False
    )
```
